32 devices in a mesh: pipe: 4 (over z), ctx: 8 (over y, x, core).
Axes of the slice: x: 2, y: 2, z: 4, core: 2. Of those that a mesh axis runs over, the one named last changes fastest.
Arguments:
- query_projections: bfloat16 [4, 1024, 4096], P('pipe', 'ctx'), may hold values from -300 to 300
- key_states: bfloat16 [4, 1024, 512], P('pipe', 'ctx'), may hold values from -7 to 7
- value_projections: bfloat16 [4, 1024, 512], P('pipe', 'ctx'), may hold values from -6 to 6
- grad_incoming: bfloat16 [4, 1024, 4096], P('pipe', 'ctx'), may hold values from -6 to 6
- key_blocks: int32 [4, 16, 2], P('pipe', 'ctx'), may hold values from -1 to 15, as said below
Outputs:
- query_gradient: bfloat16 [4, 1024, 4096], P('pipe', 'ctx')
- key_gradient: bfloat16 [4, 1024, 512], P('pipe', 'ctx')
The draws below stay inside these ranges and needn't reach their ends.
Inputs may be any that keep to these rules, and one draw needn't show every extreme that they name: `key_blocks`: entry 0 of every list is the query block itself. Each later entry is the parent of the one before (every block's parent lies 1 to 4 blocks before it), or -1 once a root was passed, and stays -1 after. No listed block lies on a device of ctx more than 2 devices before its query block's device, and in every draw some listed block lies exactly 2 devices before.
All inputs are finite; a program needn't handle non-finite values.
Results may differ from the reference program's by a relative error of at most 0.013.
Values may be sent and summed in bfloat16 or wider, within the bound.
A program may use at most 64 MiB of HBM per device.

```python
import jax
import jax.numpy as jnp
from jax import lax

QUERY_HEADS = 32
KEY_VALUE_HEADS = 4
HEAD_SIZE = 128
TREE_BLOCK_SIZE = 64
MAXB = 2
DMAX = 4
QUERY_GROUP = 8
BLOCKS_PER_RANK = 2
CASCADE_PARTS = 4
TOKEN_COUNT = 1024
NBLK = 16


def closing_keys(key):
    sampled_blocks = jnp.clip(jax.random.normal(jax.random.fold_in(key, 11), (CASCADE_PARTS, TOKEN_COUNT, KEY_VALUE_HEADS * HEAD_SIZE), jnp.float32), -6.0, 6.0)
    return sampled_blocks


def draw_key_states(key, part):
    return closing_keys(key).astype(jnp.bfloat16)


def draw_query_projections(key, part):
    sampled_blocks = jnp.clip(jax.random.normal(jax.random.fold_in(key, 15), (CASCADE_PARTS, TOKEN_COUNT, QUERY_HEADS * HEAD_SIZE), jnp.float32), -6.0, 6.0)
    return sampled_blocks.astype(jnp.bfloat16)


def draw_key_blocks(key, part):
    blocks = jnp.arange(NBLK, dtype=jnp.int32)[None, :]
    spacing = jax.random.randint(jax.random.fold_in(key, 21), (CASCADE_PARTS, NBLK), 1, DMAX + 1)
    starts = jax.random.randint(jax.random.fold_in(key, 22), (CASCADE_PARTS, NBLK), 0, 5) == 0
    parent = jnp.where(starts | (blocks < spacing), -1, blocks - spacing)
    anchor = NBLK - BLOCKS_PER_RANK
    forced = (blocks <= anchor) & (blocks > anchor - (MAXB - 1) * DMAX) & ((anchor - blocks) % DMAX == 0)
    parent = jnp.where(forced, blocks - DMAX, parent).astype(jnp.int32)
    current = jnp.broadcast_to(blocks, (CASCADE_PARTS, NBLK))
    lineage = [current]
    for stepper in range(MAXB - 1):
        upper = jnp.take_along_axis(parent, jnp.maximum(current, 0), axis=1)
        current = jnp.where(current >= 0, upper, -1)
        lineage.append(current)
    return jnp.stack(lineage, axis=-1).astype(jnp.int32)


def levels(stream_key, shape, pieces, smallest, top_value):
    def one(position, parts):
        heights = jax.random.uniform(jax.random.fold_in(jax.random.fold_in(stream_key, 6), position), (parts,), jnp.float32, smallest / len(pieces), top_value / len(pieces))
        return jnp.repeat(jnp.exp(heights), shape[position] // parts).reshape((-1,) + (1,) * (len(shape) - position - 1))

    gain = one(*pieces[0])
    for cut in pieces[1:]:
        gain = gain * one(*cut)
    return gain


def noise(key, extent, scale, reach, split=(), kind=jnp.bfloat16):
    gain = levels(key, extent, split, -0.22, 0.18) if split else 1.0
    values = jax.random.normal(key, extent, jnp.float32) * scale * gain
    return jnp.minimum(jnp.maximum(values, -reach), reach).astype(kind)


def setup_inputs(seed: int = 0) -> dict:
    arg_keys = jax.random.split(jax.random.key(seed), 6)
    return {
        "query_projections": draw_query_projections(jax.random.fold_in(arg_keys[5], 71), 0),
        "key_states": draw_key_states(jax.random.fold_in(arg_keys[5], 71), 0),
        "value_projections": noise(arg_keys[2], (CASCADE_PARTS, TOKEN_COUNT, KEY_VALUE_HEADS * HEAD_SIZE), 1.0, 6.0, ((0, 4), (1, 8))),
        "grad_incoming": noise(arg_keys[3], (CASCADE_PARTS, TOKEN_COUNT, QUERY_HEADS * HEAD_SIZE), 1.0, 6.0, ((0, 4), (1, 8))),
        "key_blocks": draw_key_blocks(jax.random.fold_in(arg_keys[5], 71), 0),
    }


def block_terms(query_blk, key_sel, value_sel, grad_blk, entries, first_pos):
    listed = entries >= 0
    clamped = jnp.maximum(entries, 0)
    query_pos = first_pos + jnp.arange(query_blk.shape[0], dtype=jnp.int32)
    key_pos = clamped[:, None] * key_sel.shape[1] + jnp.arange(key_sel.shape[1], dtype=jnp.int32)[None, :]
    allowed = listed[None, :, None] & (key_pos[None, :, :] <= query_pos[:, None, None])
    inverse_root = query_blk.shape[-1] ** -0.5
    query_f = query_blk.astype(jnp.float32)
    key_f = key_sel.astype(jnp.float32)
    value_f = value_sel.astype(jnp.float32)
    grad_f = grad_blk.astype(jnp.float32)
    scores = jnp.einsum('qhgd,jkhd->hgqjk', query_f, key_f) * inverse_root
    scores = jnp.where(allowed[None, None], scores, -1e30)
    row_max = jnp.max(scores, axis=(3, 4), keepdims=True)
    weights = jnp.exp(scores - row_max)
    softmax = weights / jnp.sum(weights, axis=(3, 4), keepdims=True)
    softmax_lo = lax.optimization_barrier(softmax.astype(jnp.bfloat16)).astype(jnp.float32)
    attended = jnp.einsum('hgqjk,jkhd->qhgd', softmax_lo, value_f).astype(jnp.bfloat16)
    attended_f = lax.optimization_barrier(attended).astype(jnp.float32)
    row_dot = jnp.einsum('qhgd,qhgd->hgq', grad_f, attended_f)
    dprob = jnp.einsum('qhgd,jkhd->hgqjk', grad_f, value_f)
    dscore = (softmax * (dprob - row_dot[..., None, None])).astype(jnp.bfloat16)
    dscore_f = lax.optimization_barrier(dscore).astype(jnp.float32)
    query_gradient = (jnp.einsum('hgqjk,jkhd->qhgd', dscore_f, key_f) * inverse_root).astype(jnp.bfloat16)
    grad_key_ent = jnp.einsum('hgqjk,qhgd->jkhd', dscore_f, query_f) * inverse_root
    entry_mask = listed[:, None, None, None]
    return query_gradient, jnp.where(entry_mask, grad_key_ent, 0.0)


def section_terms(operands):
    section_queries, section_keys, section_values, section_gradient, entries_s = operands
    block_count = entries_s.shape[0]
    query_block_rows = section_queries.reshape(block_count, TREE_BLOCK_SIZE, KEY_VALUE_HEADS, QUERY_GROUP, HEAD_SIZE)
    gradient_blocks = section_gradient.reshape(block_count, TREE_BLOCK_SIZE, KEY_VALUE_HEADS, QUERY_GROUP, HEAD_SIZE)
    section_key_blocks = section_keys.reshape(block_count, TREE_BLOCK_SIZE, KEY_VALUE_HEADS, HEAD_SIZE)
    section_value_blocks = section_values.reshape(block_count, TREE_BLOCK_SIZE, KEY_VALUE_HEADS, HEAD_SIZE)

    def single_block(block_index):
        entries = entries_s[block_index]
        clamped = jnp.maximum(entries, 0)
        return block_terms(query_block_rows[block_index], section_key_blocks[clamped], section_value_blocks[clamped],
                           gradient_blocks[block_index], entries, block_index * TREE_BLOCK_SIZE)

    query_gradient, key_contributions = lax.map(single_block, jnp.arange(block_count, dtype=jnp.int32))
    target_blocks = jnp.maximum(entries_s, 0).reshape(-1)
    key_gradient = jnp.zeros((block_count, TREE_BLOCK_SIZE, KEY_VALUE_HEADS, HEAD_SIZE), jnp.float32).at[target_blocks].add(key_contributions.reshape(-1, TREE_BLOCK_SIZE, KEY_VALUE_HEADS, HEAD_SIZE))
    selected_rows = block_count * TREE_BLOCK_SIZE
    return (query_gradient.reshape(selected_rows, QUERY_HEADS * HEAD_SIZE), key_gradient.astype(jnp.bfloat16).reshape(selected_rows, KEY_VALUE_HEADS * HEAD_SIZE))


def reference(query_projections, key_states, value_projections, grad_incoming, key_blocks):
    output_gradient = jnp.roll(grad_incoming, -1, axis=0)
    query_gradient, key_gradient = lax.map(
        section_terms, (query_projections, key_states, value_projections, output_gradient, key_blocks))
    return (query_gradient, key_gradient)
```

```python
import functools

import jax
import jax.numpy as jnp
from jax import lax
from jax.experimental import pallas as pl
from jax.experimental.pallas import tpu as pltpu
from jax.sharding import PartitionSpec as P

HEADS = 32
GROUPS = 4
SIZE = 128
BLOCK = 64
SHARE = 8
BLOCKS = 2
REACH = 2
MESH = pl.DeviceIdType.MESH
NEG = -1e30


def stacked(ref, block, group):
    rows = pl.ds(block * BLOCK, BLOCK)
    return jnp.concatenate(
        [
            ref[rows, pl.ds(pl.multiple_of(group * SHARE * SIZE, SIZE) + h * SIZE, SIZE)]
            for h in range(SHARE)
        ],
        axis=0,
    )


def nt(a, b):
    return lax.dot_general(a, b, (((1,), (1,)), ((), ())), preferred_element_type=jnp.float32)


def tn(a, b):
    return lax.dot_general(a, b, (((0,), (0,)), ((), ())), preferred_element_type=jnp.float32)


def kernel(
    pipes, ranks, entries, q_hbm, k_hbm, v_hbm, g_hbm, dq_hbm, dk_hbm,
    qbuf, gbuf, kwin, vwin, kpar, vpar, prob, dqbuf, own, msg, arrived, dkbuf,
    load_sem, halo_send, halo_recv, grad_send, grad_recv, msg_send, msg_recv, out_sem,
):
    pipe = lax.axis_index("pipe")
    rank = lax.axis_index("ctx")
    rows = BLOCKS * BLOCK
    narrow = GROUPS * SIZE
    scale = SIZE**-0.5

    def ctx_at(step):
        return (pipe, lax.rem(rank + step + ranks, ranks))

    def pipe_at(step):
        return (lax.rem(pipe + step + pipes, pipes), rank)

    barrier = pltpu.get_barrier_semaphore()
    peers = [pipe_at(-1), pipe_at(1), ctx_at(1), ctx_at(2), ctx_at(-1), ctx_at(-2)]
    for peer in peers:
        pl.semaphore_signal(barrier, inc=1, device_id=peer, device_id_type=MESH)

    last = pl.ds(REACH * rows, rows)
    loads = [
        pltpu.make_async_copy(q_hbm, qbuf, load_sem.at[0]),
        pltpu.make_async_copy(k_hbm, kwin.at[last], load_sem.at[1]),
        pltpu.make_async_copy(v_hbm, vwin.at[last], load_sem.at[2]),
    ]
    for load in loads:
        load.start()
    pl.semaphore_wait(barrier, len(peers))

    halos = []
    for reach in (1, 2):
        place = pl.ds((REACH - reach) * rows, rows)
        for which, (source, window) in enumerate(((k_hbm, kwin), (v_hbm, vwin))):
            halos.append(
                pltpu.make_async_remote_copy(
                    src_ref=source,
                    dst_ref=window.at[place],
                    send_sem=halo_send.at[reach - 1, which],
                    recv_sem=halo_recv.at[reach - 1, which],
                    device_id=ctx_at(reach),
                    device_id_type=MESH,
                )
            )

    def grad_copy(group, block):
        part = pl.ds(block * BLOCK, BLOCK)
        lanes = pl.ds(group * SHARE * SIZE, SHARE * SIZE)
        return pltpu.make_async_remote_copy(
            src_ref=g_hbm.at[part, lanes],
            dst_ref=gbuf.at[part, lanes],
            send_sem=grad_send.at[group, block],
            recv_sem=grad_recv.at[group, block],
            device_id=pipe_at(-1),
            device_id_type=MESH,
        )

    def msg_copy(group, reach):
        return pltpu.make_async_remote_copy(
            src_ref=msg.at[reach - 1, group],
            dst_ref=arrived.at[reach - 1, group],
            send_sem=msg_send.at[reach - 1, group],
            recv_sem=msg_recv.at[reach - 1, group],
            device_id=ctx_at(-reach),
            device_id_type=MESH,
        )

    grads = [[grad_copy(group, block) for block in range(BLOCKS)] for group in range(GROUPS)]
    grads[0][0].start()
    for halo in halos:
        halo.start()
    for group in range(GROUPS):
        for block in range(BLOCKS):
            if (group, block) != (0, 0):
                grads[group][block].start()
    for load in loads:
        load.wait()
    for halo in halos:
        halo.wait_recv()

    def slot_of(block, shape):
        entry = jnp.full(shape, entries[block, 1], jnp.int32)
        return jnp.where(entry >= 0, entry - (rank - REACH) * BLOCKS, -1)

    for block in range(BLOCKS):
        wide = slot_of(block, (BLOCK, narrow))
        for window, parents in ((kwin, kpar), (vwin, vpar)):
            total = jnp.zeros((BLOCK, narrow), jnp.float32)
            for slot in range(block, REACH * BLOCKS + block):
                held = window[pl.ds(slot * BLOCK, BLOCK), :].astype(jnp.float32)
                total = jnp.where(wide == slot, held, total)
            parents[block] = total.astype(jnp.bfloat16)

    def chosen(window, parents, group, block):
        lanes = pl.ds(pl.multiple_of(group * SIZE, SIZE), SIZE)
        mine = window[pl.ds(REACH * rows + block * BLOCK, BLOCK), lanes]
        return jnp.concatenate([mine, parents[block, :, lanes]], axis=0)

    slots = [slot_of(block, (BLOCK, SIZE)) for block in range(BLOCKS)]
    width = SHARE * BLOCK
    key_row = lax.broadcasted_iota(jnp.int32, (BLOCK, width), 0)
    query_row = lax.rem(lax.broadcasted_iota(jnp.int32, (BLOCK, width), 1), BLOCK)

    def forward(group, carry):
        for block in range(BLOCKS):
            scores = nt(chosen(kwin, kpar, group, block), stacked(qbuf, block, group))
            mine = jnp.where(key_row <= query_row, scores[:BLOCK], NEG)
            parent = jnp.where(slot_of(block, (BLOCK, width)) >= 0, scores[BLOCK:], NEG)
            top = jnp.maximum(
                jnp.max(mine, axis=0, keepdims=True), jnp.max(parent, axis=0, keepdims=True)
            )
            mine = jnp.exp((mine - top) * scale)
            parent = jnp.exp((parent - top) * scale)
            total = jnp.sum(mine, axis=0, keepdims=True) + jnp.sum(parent, axis=0, keepdims=True)
            inverse = 1.0 / total
            prob[group, block, :BLOCK] = mine * inverse
            prob[group, block, BLOCK:] = parent * inverse
        return carry

    lax.fori_loop(0, GROUPS, forward, 0)

    def backward(group, block):
        soft = prob[group, block]
        dprob = nt(chosen(vwin, vpar, group, block), stacked(gbuf, block, group))
        dot = jnp.sum(soft * dprob, axis=0, keepdims=True)
        dscore = (soft * (dprob - dot)).astype(jnp.bfloat16)
        dkey = (
            jnp.dot(dscore, stacked(qbuf, block, group), preferred_element_type=jnp.float32) * scale
        )
        return dscore, dkey

    def query_part(group, block, dscore):
        dquery = (tn(dscore, chosen(kwin, kpar, group, block)) * scale).astype(jnp.bfloat16)
        for h in range(SHARE):
            dqbuf[pl.ds(block * BLOCK, BLOCK), pl.ds((group * SHARE + h) * SIZE, SIZE)] = dquery[
                h * BLOCK : (h + 1) * BLOCK
            ]

    writes = []

    def write_query(group, block):
        part = pl.ds(block * BLOCK, BLOCK)
        lanes = pl.ds(group * SHARE * SIZE, SHARE * SIZE)
        write = pltpu.make_async_copy(
            dqbuf.at[part, lanes], dq_hbm.at[part, lanes], out_sem.at[group * BLOCKS + block]
        )
        write.start()
        writes.append(write)

    for group in range(GROUPS):
        grads[group][0].wait_recv()
        dscore0, dkey0 = backward(group, 0)
        query_part(group, 0, dscore0)
        write_query(group, 0)
        grads[group][1].wait_recv()
        dscore1, dkey1 = backward(group, 1)
        parent0, parent1 = dkey0[BLOCK:], dkey1[BLOCK:]

        def at_slot(slot):
            total = jnp.zeros((BLOCK, SIZE), jnp.float32)
            for block, parent in enumerate((parent0, parent1)):
                if block <= slot < REACH * BLOCKS + block:
                    total = total + jnp.where(slots[block] == slot, parent, 0.0)
            return total

        for reach in (2, 1):
            first = (REACH - reach) * BLOCKS
            for block in range(BLOCKS):
                msg[reach - 1, group, pl.ds(block * BLOCK, BLOCK)] = at_slot(first + block).astype(
                    jnp.bfloat16
                )
            msg_copy(group, reach).start()
        own[group, :BLOCK] = dkey0[:BLOCK] + at_slot(REACH * BLOCKS)
        own[group, BLOCK:] = dkey1[:BLOCK]
        query_part(group, 1, dscore1)
        write_query(group, 1)

    for group in range(GROUPS):
        total = own[group]
        for reach in (1, 2):
            msg_copy(group, reach).wait_recv()
            total = total + arrived[reach - 1, group].astype(jnp.float32)
        dkbuf[:, pl.ds(group * SIZE, SIZE)] = total.astype(jnp.bfloat16)
    write = pltpu.make_async_copy(dkbuf, dk_hbm, out_sem.at[GROUPS * BLOCKS])
    write.start()
    writes.append(write)

    for halo in halos:
        halo.wait_send()
    for group in range(GROUPS):
        for block in range(BLOCKS):
            grads[group][block].wait_send()
        for reach in (1, 2):
            msg_copy(group, reach).wait_send()
    for write in writes:
        write.wait()


def solution(mesh):
    pipes, ranks = mesh.shape["pipe"], mesh.shape["ctx"]

    def per_device(query, key, value, grad, key_blocks):
        rows = query.shape[1]
        wide, narrow = query.shape[2], key.shape[2]
        anywhere = pl.BlockSpec(memory_space=pl.ANY)
        dma = pltpu.SemaphoreType.DMA
        dq, dk = pl.pallas_call(
            functools.partial(kernel, pipes, ranks),
            out_shape=(
                jax.ShapeDtypeStruct((rows, wide), jnp.bfloat16),
                jax.ShapeDtypeStruct((rows, narrow), jnp.bfloat16),
            ),
            in_specs=[pl.BlockSpec(memory_space=pltpu.SMEM)] + [anywhere] * 4,
            out_specs=(anywhere, anywhere),
            scratch_shapes=[
                pltpu.VMEM((rows, wide), jnp.bfloat16),
                pltpu.VMEM((rows, wide), jnp.bfloat16),
                pltpu.VMEM(((REACH + 1) * rows, narrow), jnp.bfloat16),
                pltpu.VMEM(((REACH + 1) * rows, narrow), jnp.bfloat16),
                pltpu.VMEM((BLOCKS, BLOCK, narrow), jnp.bfloat16),
                pltpu.VMEM((BLOCKS, BLOCK, narrow), jnp.bfloat16),
                pltpu.VMEM((GROUPS, BLOCKS, 2 * BLOCK, SHARE * BLOCK), jnp.float32),
                pltpu.VMEM((rows, wide), jnp.bfloat16),
                pltpu.VMEM((GROUPS, rows, SIZE), jnp.float32),
                pltpu.VMEM((REACH, GROUPS, rows, SIZE), jnp.bfloat16),
                pltpu.VMEM((REACH, GROUPS, rows, SIZE), jnp.bfloat16),
                pltpu.VMEM((rows, narrow), jnp.bfloat16),
                dma((3,)),
                dma((REACH, 2)),
                dma((REACH, 2)),
                dma((GROUPS, BLOCKS)),
                dma((GROUPS, BLOCKS)),
                dma((REACH, GROUPS)),
                dma((REACH, GROUPS)),
                dma((GROUPS * BLOCKS + 1,)),
            ],
            compiler_params=pltpu.CompilerParams(
                collective_id=0, has_side_effects=True, vmem_limit_bytes=32 * 1024 * 1024
            ),
            cost_estimate=pl.CostEstimate(
                flops=700_000_000, bytes_accessed=4_000_000, transcendentals=600_000
            ),
        )(key_blocks[0], query[0], key[0], value[0], grad[0])
        return dq[None], dk[None]

    spec = P("pipe", "ctx", None)
    return jax.shard_map(
        per_device, mesh=mesh, in_specs=(spec,) * 5, out_specs=(spec, spec), check_vma=False
    )
```

```python
import functools

import jax
import jax.numpy as jnp
from jax import lax
from jax.experimental import pallas as pl
from jax.experimental.pallas import tpu as pltpu
from jax.sharding import PartitionSpec as P

HEADS = 32
GROUPS = 4
SIZE = 128
BLOCK = 64
SHARE = 8
BLOCKS = 2
REACH = 2
MESH = pl.DeviceIdType.MESH
NEG = -1e30
PIECES = [(g, b, 0, SHARE) for g in range(GROUPS) for b in range(BLOCKS)][:-1]
PIECES += [(GROUPS - 1, BLOCKS - 1, 0, 4), (GROUPS - 1, BLOCKS - 1, 4, 2), (GROUPS - 1, BLOCKS - 1, 6, 2)]


def stacked(ref, block, group, first=0, heads=SHARE):
    rows = pl.ds(block * BLOCK, BLOCK)
    return jnp.concatenate(
        [
            ref[rows, pl.ds(pl.multiple_of(group * SHARE * SIZE, SIZE) + h * SIZE, SIZE)]
            for h in range(first, first + heads)
        ],
        axis=0,
    )


def nt(a, b):
    return lax.dot_general(a, b, (((1,), (1,)), ((), ())), preferred_element_type=jnp.float32)


def tn(a, b):
    return lax.dot_general(a, b, (((0,), (0,)), ((), ())), preferred_element_type=jnp.float32)


def kernel(
    pipes, ranks, e_hbm, q_hbm, k_hbm, v_hbm, g_hbm, dq_hbm, dk_hbm,
    entries, qbuf, gbuf, kwin, vwin, kpar, vpar, prob, dqbuf, own, msg, arrived, dkbuf,
    load_sem, halo_send, halo_recv, grad_send, grad_recv, msg_send, msg_recv, out_sem,
):
    pipe = lax.axis_index("pipe")
    rank = lax.axis_index("ctx")
    rows = BLOCKS * BLOCK
    narrow = GROUPS * SIZE
    scale = SIZE**-0.5

    def ctx_at(step):
        return (pipe, lax.rem(rank + step + ranks, ranks))

    def pipe_at(step):
        return (lax.rem(pipe + step + pipes, pipes), rank)

    barrier = pltpu.get_barrier_semaphore()
    peers = [pipe_at(-1), pipe_at(1), ctx_at(1), ctx_at(2), ctx_at(-1), ctx_at(-2)]
    for peer in peers:
        pl.semaphore_signal(barrier, inc=1, device_id=peer, device_id_type=MESH)

    last = pl.ds(REACH * rows, rows)
    loads = [
        pltpu.make_async_copy(q_hbm, qbuf, load_sem.at[0]),
        pltpu.make_async_copy(k_hbm, kwin.at[last], load_sem.at[1]),
        pltpu.make_async_copy(v_hbm, vwin.at[last], load_sem.at[2]),
        pltpu.make_async_copy(e_hbm, entries, load_sem.at[3]),
    ]
    for load in loads:
        load.start()
    pl.semaphore_wait(barrier, len(peers))

    halos = []
    for reach in (1, 2):
        place = pl.ds((REACH - reach) * rows, rows)
        for which, (source, window) in enumerate(((k_hbm, kwin), (v_hbm, vwin))):
            halos.append(
                pltpu.make_async_remote_copy(
                    src_ref=source,
                    dst_ref=window.at[place],
                    send_sem=halo_send.at[reach - 1, which],
                    recv_sem=halo_recv.at[reach - 1, which],
                    device_id=ctx_at(reach),
                    device_id_type=MESH,
                )
            )

    def place_of(piece):
        group, block, first, heads = piece
        return pl.ds(block * BLOCK, BLOCK), pl.ds((group * SHARE + first) * SIZE, heads * SIZE)

    def grad_copy(index):
        part, lanes = place_of(PIECES[index])
        return pltpu.make_async_remote_copy(
            src_ref=g_hbm.at[part, lanes],
            dst_ref=gbuf.at[part, lanes],
            send_sem=grad_send.at[index],
            recv_sem=grad_recv.at[index],
            device_id=pipe_at(-1),
            device_id_type=MESH,
        )

    def msg_copy(group, reach):
        return pltpu.make_async_remote_copy(
            src_ref=msg.at[reach - 1, group],
            dst_ref=arrived.at[reach - 1, group],
            send_sem=msg_send.at[reach - 1, group],
            recv_sem=msg_recv.at[reach - 1, group],
            device_id=ctx_at(-reach),
            device_id_type=MESH,
        )

    grads = [grad_copy(index) for index in range(len(PIECES))]
    grads[0].start()
    for halo in halos:
        halo.start()
    for grad in grads[1:]:
        grad.start()
    for load in loads:
        load.wait()
    for halo in halos:
        halo.wait_recv()

    def slot_of(block, shape):
        entry = jnp.full(shape, entries[block, 1], jnp.int32)
        return jnp.where(entry >= 0, entry - (rank - REACH) * BLOCKS, -1)

    for block in range(BLOCKS):
        wide = slot_of(block, (BLOCK, narrow))
        for window, parents in ((kwin, kpar), (vwin, vpar)):
            total = jnp.zeros((BLOCK, narrow), jnp.float32)
            for slot in range(block, REACH * BLOCKS + block):
                held = window[pl.ds(slot * BLOCK, BLOCK), :].astype(jnp.float32)
                total = jnp.where(wide == slot, held, total)
            parents[block] = total.astype(jnp.bfloat16)

    def chosen(window, parents, group, block):
        lanes = pl.ds(pl.multiple_of(group * SIZE, SIZE), SIZE)
        mine = window[pl.ds(REACH * rows + block * BLOCK, BLOCK), lanes]
        return jnp.concatenate([mine, parents[block, :, lanes]], axis=0)

    slots = [slot_of(block, (BLOCK, SIZE)) for block in range(BLOCKS)]
    width = SHARE * BLOCK
    key_row = lax.broadcasted_iota(jnp.int32, (BLOCK, width), 0)
    query_row = lax.rem(lax.broadcasted_iota(jnp.int32, (BLOCK, width), 1), BLOCK)

    def forward(group, carry):
        for block in range(BLOCKS):
            scores = nt(chosen(kwin, kpar, group, block), stacked(qbuf, block, group))
            mine = jnp.where(key_row <= query_row, scores[:BLOCK], NEG)
            parent = jnp.where(slot_of(block, (BLOCK, width)) >= 0, scores[BLOCK:], NEG)
            top = jnp.maximum(
                jnp.max(mine, axis=0, keepdims=True), jnp.max(parent, axis=0, keepdims=True)
            )
            mine = jnp.exp((mine - top) * scale)
            parent = jnp.exp((parent - top) * scale)
            total = jnp.sum(mine, axis=0, keepdims=True) + jnp.sum(parent, axis=0, keepdims=True)
            inverse = 1.0 / total
            prob[group, block, :BLOCK] = mine * inverse
            prob[group, block, BLOCK:] = parent * inverse
        return carry

    lax.fori_loop(0, GROUPS, forward, 0)

    def backward(piece):
        group, block, first, heads = piece
        soft = prob[group, block, :, pl.ds(first * BLOCK, heads * BLOCK)]
        dprob = nt(chosen(vwin, vpar, group, block), stacked(gbuf, block, group, first, heads))
        dot = jnp.sum(soft * dprob, axis=0, keepdims=True)
        dscore = (soft * (dprob - dot)).astype(jnp.bfloat16)
        queries = stacked(qbuf, block, group, first, heads)
        return dscore, jnp.dot(dscore, queries, preferred_element_type=jnp.float32) * scale

    def query_part(piece, dscore):
        group, block, first, heads = piece
        dquery = (tn(dscore, chosen(kwin, kpar, group, block)) * scale).astype(jnp.bfloat16)
        for h in range(heads):
            dqbuf[pl.ds(block * BLOCK, BLOCK), pl.ds((group * SHARE + first + h) * SIZE, SIZE)] = (
                dquery[h * BLOCK : (h + 1) * BLOCK]
            )

    writes = []

    def write_query(index):
        part, lanes = place_of(PIECES[index])
        write = pltpu.make_async_copy(
            dqbuf.at[part, lanes], dq_hbm.at[part, lanes], out_sem.at[index]
        )
        write.start()
        writes.append(write)

    totals = {}
    for index, piece in enumerate(PIECES):
        group, block = piece[:2]
        grads[index].wait_recv()
        dscore, dkey = backward(piece)
        totals[group, block] = totals[group, block] + dkey if (group, block) in totals else dkey
        if index + 1 == len(PIECES) or PIECES[index + 1][0] != group:
            parents = [totals[group, other][BLOCK:] for other in range(BLOCKS)]

            def at_slot(slot):
                total = jnp.zeros((BLOCK, SIZE), jnp.float32)
                for other, parent in enumerate(parents):
                    if other <= slot < REACH * BLOCKS + other:
                        total = total + jnp.where(slots[other] == slot, parent, 0.0)
                return total

            for reach in (2, 1):
                begin = (REACH - reach) * BLOCKS
                for other in range(BLOCKS):
                    msg[reach - 1, group, pl.ds(other * BLOCK, BLOCK)] = at_slot(
                        begin + other
                    ).astype(jnp.bfloat16)
                msg_copy(group, reach).start()
            own[group, :BLOCK] = totals[group, 0][:BLOCK] + at_slot(REACH * BLOCKS)
            own[group, BLOCK:] = totals[group, 1][:BLOCK]
        query_part(piece, dscore)
        write_query(index)

    for halo in halos:
        halo.wait_send()
    for grad in grads:
        grad.wait_send()
    for group in range(GROUPS):
        total = own[group]
        for reach in (1, 2):
            msg_copy(group, reach).wait_recv()
            total = total + arrived[reach - 1, group].astype(jnp.float32)
        dkbuf[:, pl.ds(group * SIZE, SIZE)] = total.astype(jnp.bfloat16)
    write = pltpu.make_async_copy(dkbuf, dk_hbm, out_sem.at[len(PIECES)])
    write.start()
    writes.append(write)
    for group in range(GROUPS):
        for reach in (1, 2):
            msg_copy(group, reach).wait_send()
    for write in writes:
        write.wait()


def finish(dq_in, dk_in, dq_out, dk_out, sem):
    copies = [
        pltpu.make_async_copy(dq_in, dq_out, sem.at[0]),
        pltpu.make_async_copy(dk_in, dk_out, sem.at[1]),
    ]
    for copy in copies:
        copy.start()
    for copy in copies:
        copy.wait()


def solution(mesh):
    pipes, ranks = mesh.shape["pipe"], mesh.shape["ctx"]

    def per_device(query, key, value, grad, key_blocks):
        rows = query.shape[1]
        wide, narrow = query.shape[2], key.shape[2]
        anywhere = pl.BlockSpec(memory_space=pl.ANY)
        dma = pltpu.SemaphoreType.DMA
        dq, dk = pl.pallas_call(
            functools.partial(kernel, pipes, ranks),
            out_shape=(
                jax.ShapeDtypeStruct((rows, wide), jnp.bfloat16),
                jax.ShapeDtypeStruct((rows, narrow), jnp.bfloat16),
            ),
            in_specs=[pl.BlockSpec(memory_space=pltpu.HBM)] * 5,
            out_specs=(anywhere, anywhere),
            scratch_shapes=[
                pltpu.SMEM((BLOCKS, 2), jnp.int32),
                pltpu.VMEM((rows, wide), jnp.bfloat16),
                pltpu.VMEM((rows, wide), jnp.bfloat16),
                pltpu.VMEM(((REACH + 1) * rows, narrow), jnp.bfloat16),
                pltpu.VMEM(((REACH + 1) * rows, narrow), jnp.bfloat16),
                pltpu.VMEM((BLOCKS, BLOCK, narrow), jnp.bfloat16),
                pltpu.VMEM((BLOCKS, BLOCK, narrow), jnp.bfloat16),
                pltpu.VMEM((GROUPS, BLOCKS, 2 * BLOCK, SHARE * BLOCK), jnp.float32),
                pltpu.VMEM((rows, wide), jnp.bfloat16),
                pltpu.VMEM((GROUPS, rows, SIZE), jnp.float32),
                pltpu.VMEM((REACH, GROUPS, rows, SIZE), jnp.bfloat16),
                pltpu.VMEM((REACH, GROUPS, rows, SIZE), jnp.bfloat16),
                pltpu.VMEM((rows, narrow), jnp.bfloat16),
                dma((4,)),
                dma((REACH, 2)),
                dma((REACH, 2)),
                dma((len(PIECES),)),
                dma((len(PIECES),)),
                dma((REACH, GROUPS)),
                dma((REACH, GROUPS)),
                dma((len(PIECES) + 1,)),
            ],
            compiler_params=pltpu.CompilerParams(
                collective_id=0, has_side_effects=True, vmem_limit_bytes=32 * 1024 * 1024
            ),
            cost_estimate=pl.CostEstimate(
                flops=700_000_000, bytes_accessed=4_000_000, transcendentals=600_000
            ),
        )(*[pltpu.with_memory_space_constraint(x[0], pltpu.HBM) for x in (key_blocks, query, key, value, grad)])
        dq, dk = pl.pallas_call(
            finish,
            out_shape=(
                jax.ShapeDtypeStruct((rows, wide), jnp.bfloat16),
                jax.ShapeDtypeStruct((rows, narrow), jnp.bfloat16),
            ),
            in_specs=[anywhere] * 2,
            out_specs=[pl.BlockSpec(memory_space=pltpu.HBM)] * 2,
            scratch_shapes=[dma((2,))],
            compiler_params=pltpu.CompilerParams(vmem_limit_bytes=4 * 1024 * 1024),
        )(*[pltpu.with_memory_space_constraint(x, pltpu.VMEM) for x in (dq, dk)])
        return dq[None], dk[None]

    spec = P("pipe", "ctx", None)
    return jax.shard_map(
        per_device, mesh=mesh, in_specs=(spec,) * 5, out_specs=(spec, spec), check_vma=False
    )
```

```python
import functools

import jax
import jax.numpy as jnp
from jax import lax
from jax.experimental import pallas as pl
from jax.experimental.pallas import tpu as pltpu
from jax.sharding import PartitionSpec as P

HEADS = 32
GROUPS = 4
SIZE = 128
BLOCK = 64
SHARE = 8
BLOCKS = 2
REACH = 2
MESH = pl.DeviceIdType.MESH
NEG = -1e30
CUTS = 1
PIECES = [(g, b, 0, SHARE) for g in range(GROUPS) for b in range(BLOCKS)][:-1]
PIECES += [(GROUPS - 1, BLOCKS - 1, 0, 4), (GROUPS - 1, BLOCKS - 1, 4, 2), (GROUPS - 1, BLOCKS - 1, 6, 2)]


def stacked(ref, block, group, first=0, heads=SHARE):
    rows = pl.ds(block * BLOCK, BLOCK)
    return jnp.concatenate(
        [
            ref[rows, pl.ds(pl.multiple_of(group * SHARE * SIZE, SIZE) + h * SIZE, SIZE)]
            for h in range(first, first + heads)
        ],
        axis=0,
    )


def nt(a, b):
    return lax.dot_general(a, b, (((1,), (1,)), ((), ())), preferred_element_type=jnp.float32)


def tn(a, b):
    return lax.dot_general(a, b, (((0,), (0,)), ((), ())), preferred_element_type=jnp.float32)


def kernel(
    pipes, ranks, e_hbm, q_hbm, k_hbm, v_hbm, g_hbm, dq_ref, dk_ref,
    entries, qbuf, gbuf, kwin, vwin, kpar, vpar, prob, own, msg, arrived, note, notes,
    load_sem, halo_send, halo_recv, grad_send, grad_recv, msg_send, msg_recv, note_send, note_recv,
):
    pipe = lax.axis_index("pipe")
    rank = lax.axis_index("ctx")
    rows = BLOCKS * BLOCK
    narrow = GROUPS * SIZE
    scale = SIZE**-0.5

    def ctx_at(step):
        return (pipe, lax.rem(rank + step + ranks, ranks))

    def pipe_at(step):
        return (lax.rem(pipe + step + pipes, pipes), rank)

    barrier = pltpu.get_barrier_semaphore()
    peers = [pipe_at(-1), pipe_at(1), ctx_at(1), ctx_at(2), ctx_at(-1), ctx_at(-2)]
    for peer in peers:
        pl.semaphore_signal(barrier, inc=1, device_id=peer, device_id_type=MESH)

    last = pl.ds(REACH * rows, rows)
    loads = [
        pltpu.make_async_copy(q_hbm, qbuf, load_sem.at[0]),
        pltpu.make_async_copy(k_hbm, kwin.at[last], load_sem.at[1]),
        pltpu.make_async_copy(v_hbm, vwin.at[last], load_sem.at[2]),
        pltpu.make_async_copy(e_hbm, entries, load_sem.at[3]),
    ]
    for load in loads:
        load.start()
    pl.semaphore_wait(barrier, len(peers))

    halos = []
    for reach in (1, 2):
        place = pl.ds((REACH - reach) * rows, rows)
        for which, (source, window) in enumerate(((k_hbm, kwin), (v_hbm, vwin))):
            halos.append(
                pltpu.make_async_remote_copy(
                    src_ref=source,
                    dst_ref=window.at[place],
                    send_sem=halo_send.at[reach - 1, which],
                    recv_sem=halo_recv.at[reach - 1, which],
                    device_id=ctx_at(reach),
                    device_id_type=MESH,
                )
            )

    def place_of(piece):
        group, block, first, heads = piece
        return pl.ds(block * BLOCK, BLOCK), pl.ds((group * SHARE + first) * SIZE, heads * SIZE)

    def grad_copy(index):
        part, lanes = place_of(PIECES[index])
        return pltpu.make_async_remote_copy(
            src_ref=g_hbm.at[part, lanes],
            dst_ref=gbuf.at[part, lanes],
            send_sem=grad_send.at[index],
            recv_sem=grad_recv.at[index],
            device_id=pipe_at(-1),
            device_id_type=MESH,
        )

    def msg_copy(group, block, reach):
        return pltpu.make_async_remote_copy(
            src_ref=msg.at[group, block],
            dst_ref=arrived.at[reach - 1, group, block],
            send_sem=msg_send.at[reach - 1, group, block],
            recv_sem=msg_recv.at[reach - 1, group, block],
            device_id=ctx_at(-reach),
            device_id_type=MESH,
        )

    note_copies = [
        pltpu.make_async_remote_copy(
            src_ref=note,
            dst_ref=notes.at[reach - 1],
            send_sem=note_send.at[reach - 1],
            recv_sem=note_recv.at[reach - 1],
            device_id=ctx_at(-reach),
            device_id_type=MESH,
        )
        for reach in (1, 2)
    ]

    grads = [grad_copy(index) for index in range(len(PIECES))]
    grads[0].start()
    for halo in halos:
        halo.start()
    for grad in grads[1:]:
        grad.start()
    for load in loads:
        load.wait()
    for halo in halos:
        halo.wait_recv()

    def slot_of(block, shape):
        entry = jnp.full(shape, entries[block, 1], jnp.int32)
        return jnp.where(entry >= 0, entry - (rank - REACH) * BLOCKS, -1)

    for block in range(BLOCKS):
        note[block] = slot_of(block, (8, SIZE))
    for copy in note_copies:
        copy.start()

    for block in range(BLOCKS):
        wide = slot_of(block, (BLOCK, narrow))
        for window, parents in ((kwin, kpar), (vwin, vpar)):
            total = jnp.zeros((BLOCK, narrow), jnp.float32)
            for slot in range(block, REACH * BLOCKS + block):
                held = window[pl.ds(slot * BLOCK, BLOCK), :].astype(jnp.float32)
                total = jnp.where(wide == slot, held, total)
            parents[block] = total.astype(jnp.bfloat16)

    def chosen(window, parents, group, block):
        lanes = pl.ds(pl.multiple_of(group * SIZE, SIZE), SIZE)
        mine = window[pl.ds(REACH * rows + block * BLOCK, BLOCK), lanes]
        return jnp.concatenate([mine, parents[block, :, lanes]], axis=0)

    slots = [slot_of(block, (BLOCK, SIZE)) for block in range(BLOCKS)]
    width = SHARE * BLOCK
    key_row = lax.broadcasted_iota(jnp.int32, (BLOCK, width), 0)
    query_row = lax.rem(lax.broadcasted_iota(jnp.int32, (BLOCK, width), 1), BLOCK)

    def forward(group, carry):
        for block in range(BLOCKS):
            scores = nt(chosen(kwin, kpar, group, block), stacked(qbuf, block, group))
            mine = jnp.where(key_row <= query_row, scores[:BLOCK], NEG)
            parent = jnp.where(slot_of(block, (BLOCK, width)) >= 0, scores[BLOCK:], NEG)
            top = jnp.maximum(
                jnp.max(mine, axis=0, keepdims=True), jnp.max(parent, axis=0, keepdims=True)
            )
            mine = jnp.exp((mine - top) * scale)
            parent = jnp.exp((parent - top) * scale)
            total = jnp.sum(mine, axis=0, keepdims=True) + jnp.sum(parent, axis=0, keepdims=True)
            inverse = 1.0 / total
            prob[group, block, :BLOCK] = mine * inverse
            prob[group, block, BLOCK:] = parent * inverse
        return carry

    lax.fori_loop(0, GROUPS, forward, 0)

    def backward(piece):
        group, block, first, heads = piece
        soft = prob[group, block, :, pl.ds(first * BLOCK, heads * BLOCK)]
        dprob = nt(chosen(vwin, vpar, group, block), stacked(gbuf, block, group, first, heads))
        dot = jnp.sum(soft * dprob, axis=0, keepdims=True)
        dscore = (soft * (dprob - dot)).astype(jnp.bfloat16)
        queries = stacked(qbuf, block, group, first, heads)
        return dscore, jnp.dot(dscore, queries, preferred_element_type=jnp.float32) * scale

    def query_part(piece, dscore):
        group, block, first, heads = piece
        dquery = (tn(dscore, chosen(kwin, kpar, group, block)) * scale).astype(jnp.bfloat16)
        for h in range(heads):
            dq_ref[pl.ds(block * BLOCK, BLOCK), pl.ds((group * SHARE + first + h) * SIZE, SIZE)] = (
                dquery[h * BLOCK : (h + 1) * BLOCK]
            )

    def close(group):
        parts = [own[group, :BLOCK], own[group, BLOCK:]]
        for reach in range(1, REACH + 1):
            for sent in range(BLOCKS):
                msg_copy(group, sent, reach).wait_recv()
                slot = jnp.broadcast_to(notes[reach - 1, sent, :1], (BLOCK, SIZE))
                part = arrived[reach - 1, group, sent].astype(jnp.float32)
                for mine in range(BLOCKS):
                    hit = slot == (REACH - reach) * BLOCKS + mine
                    parts[mine] = parts[mine] + jnp.where(hit, part, 0.0)
        for mine in range(BLOCKS):
            dk_ref[pl.ds(mine * BLOCK, BLOCK), pl.ds(group * SIZE, SIZE)] = parts[mine].astype(
                jnp.bfloat16
            )

    totals = {}
    for index, piece in enumerate(PIECES):
        group, block = piece[:2]
        grads[index].wait_recv()
        dscore, dkey = backward(piece)
        totals[block] = totals[block] + dkey if piece[2] else dkey
        if piece[2] + piece[3] == SHARE:
            parent = totals[block][BLOCK:]
            msg[group, block] = parent.astype(jnp.bfloat16)
            for reach in (2, 1):
                msg_copy(group, block, reach).start()
            own[group, pl.ds(block * BLOCK, BLOCK)] = totals[block][:BLOCK]
            if block:
                near = jnp.where(slots[block] == REACH * BLOCKS, parent, 0.0)
                own[group, :BLOCK] = own[group, :BLOCK] + near
        query_part(piece, dscore)
        if index + 3 == len(PIECES):
            for copy in note_copies:
                copy.wait_recv()
            for earlier in range(GROUPS - 1):
                close(earlier)

    for halo in halos:
        halo.wait_send()
    for copy in note_copies:
        copy.wait_send()
    for grad in grads:
        grad.wait_send()
    for group in range(GROUPS - 1):
        for sent in range(BLOCKS):
            for reach in (1, 2):
                msg_copy(group, sent, reach).wait_send()
    close(GROUPS - 1)
    for sent in range(BLOCKS):
        for reach in (1, 2):
            msg_copy(GROUPS - 1, sent, reach).wait_send()


def finish(dq_in, dk_in, dq_out, dk_out, sem):
    rows = dq_in.shape[0] // CUTS
    copies = [pltpu.make_async_copy(dk_in, dk_out, sem.at[CUTS])]
    for cut in range(CUTS):
        part = pl.ds(cut * rows, rows)
        copies.append(pltpu.make_async_copy(dq_in.at[part], dq_out.at[part], sem.at[cut]))
    for copy in copies:
        copy.start()
    for copy in copies:
        copy.wait()


def solution(mesh):
    pipes, ranks = mesh.shape["pipe"], mesh.shape["ctx"]

    def per_device(query, key, value, grad, key_blocks):
        rows = query.shape[1]
        wide, narrow = query.shape[2], key.shape[2]
        anywhere = pl.BlockSpec(memory_space=pl.ANY)
        dma = pltpu.SemaphoreType.DMA
        dq, dk = pl.pallas_call(
            functools.partial(kernel, pipes, ranks),
            out_shape=(
                jax.ShapeDtypeStruct((rows, wide), jnp.bfloat16),
                jax.ShapeDtypeStruct((rows, narrow), jnp.bfloat16),
            ),
            in_specs=[pl.BlockSpec(memory_space=pltpu.HBM)] * 5,
            out_specs=(pl.BlockSpec(memory_space=pltpu.VMEM),) * 2,
            scratch_shapes=[
                pltpu.SMEM((BLOCKS, 2), jnp.int32),
                pltpu.VMEM((rows, wide), jnp.bfloat16),
                pltpu.VMEM((rows, wide), jnp.bfloat16),
                pltpu.VMEM(((REACH + 1) * rows, narrow), jnp.bfloat16),
                pltpu.VMEM(((REACH + 1) * rows, narrow), jnp.bfloat16),
                pltpu.VMEM((BLOCKS, BLOCK, narrow), jnp.bfloat16),
                pltpu.VMEM((BLOCKS, BLOCK, narrow), jnp.bfloat16),
                pltpu.VMEM((GROUPS, BLOCKS, 2 * BLOCK, SHARE * BLOCK), jnp.float32),
                pltpu.VMEM((GROUPS, rows, SIZE), jnp.float32),
                pltpu.VMEM((GROUPS, BLOCKS, BLOCK, SIZE), jnp.bfloat16),
                pltpu.VMEM((REACH, GROUPS, BLOCKS, BLOCK, SIZE), jnp.bfloat16),
                pltpu.VMEM((BLOCKS, 8, SIZE), jnp.int32),
                pltpu.VMEM((REACH, BLOCKS, 8, SIZE), jnp.int32),
                dma((4,)),
                dma((REACH, 2)),
                dma((REACH, 2)),
                dma((len(PIECES),)),
                dma((len(PIECES),)),
                dma((REACH, GROUPS, BLOCKS)),
                dma((REACH, GROUPS, BLOCKS)),
                dma((REACH,)),
                dma((REACH,)),
            ],
            compiler_params=pltpu.CompilerParams(
                collective_id=0, has_side_effects=True, vmem_limit_bytes=32 * 1024 * 1024
            ),
            cost_estimate=pl.CostEstimate(
                flops=700_000_000, bytes_accessed=4_000_000, transcendentals=600_000
            ),
        )(*[pltpu.with_memory_space_constraint(x[0], pltpu.HBM) for x in (key_blocks, query, key, value, grad)])
        dq, dk = pl.pallas_call(
            finish,
            out_shape=(
                jax.ShapeDtypeStruct((rows, wide), jnp.bfloat16),
                jax.ShapeDtypeStruct((rows, narrow), jnp.bfloat16),
            ),
            in_specs=[anywhere] * 2,
            out_specs=[pl.BlockSpec(memory_space=pltpu.HBM)] * 2,
            scratch_shapes=[dma((CUTS + 1,))],
            compiler_params=pltpu.CompilerParams(vmem_limit_bytes=4 * 1024 * 1024),
        )(*[pltpu.with_memory_space_constraint(x, pltpu.VMEM) for x in (dq, dk)])
        return dq[None], dk[None]

    spec = P("pipe", "ctx", None)
    return jax.shard_map(
        per_device, mesh=mesh, in_specs=(spec,) * 5, out_specs=(spec, spec), check_vma=False
    )
```

```python
import functools

import jax
import jax.numpy as jnp
from jax import lax
from jax.experimental import pallas as pl
from jax.experimental.pallas import tpu as pltpu
from jax.sharding import PartitionSpec as P

HEADS = 32
GROUPS = 4
SIZE = 128
BLOCK = 64
SHARE = 8
BLOCKS = 2
REACH = 2
MESH = pl.DeviceIdType.MESH
NEG = -1e30
CUTS = 1
PIECES = [(g, b, 0, SHARE) for g in range(GROUPS) for b in range(BLOCKS)][:-1]
PIECES += [(GROUPS - 1, BLOCKS - 1, 0, 4), (GROUPS - 1, BLOCKS - 1, 4, 4)]


def stacked(ref, block, group, first=0, heads=SHARE):
    rows = pl.ds(block * BLOCK, BLOCK)
    return jnp.concatenate(
        [
            ref[rows, pl.ds(pl.multiple_of(group * SHARE * SIZE, SIZE) + h * SIZE, SIZE)]
            for h in range(first, first + heads)
        ],
        axis=0,
    )


def nt(a, b):
    return lax.dot_general(a, b, (((1,), (1,)), ((), ())), preferred_element_type=jnp.float32)


def tn(a, b):
    return lax.dot_general(a, b, (((0,), (0,)), ((), ())), preferred_element_type=jnp.float32)


def kernel(
    pipes, ranks, e_hbm, q_hbm, k_hbm, v_hbm, g_hbm, dq_ref, dk_ref,
    entries, qbuf, gbuf, kwin, vwin, kpar, vpar, prob, own, msg, arrived, note, notes,
    load_sem, halo_send, halo_recv, grad_send, grad_recv, msg_send, msg_recv, note_send, note_recv,
):
    pipe = lax.axis_index("pipe")
    rank = lax.axis_index("ctx")
    rows = BLOCKS * BLOCK
    narrow = GROUPS * SIZE
    scale = SIZE**-0.5

    def ctx_at(step):
        return (pipe, lax.rem(rank + step + ranks, ranks))

    def pipe_at(step):
        return (lax.rem(pipe + step + pipes, pipes), rank)

    barrier = pltpu.get_barrier_semaphore()
    peers = [pipe_at(-1), pipe_at(1), ctx_at(1), ctx_at(2), ctx_at(-1), ctx_at(-2)]
    for peer in peers:
        pl.semaphore_signal(barrier, inc=1, device_id=peer, device_id_type=MESH)

    last = pl.ds(REACH * rows, rows)
    loads = [
        pltpu.make_async_copy(q_hbm, qbuf, load_sem.at[0]),
        pltpu.make_async_copy(k_hbm, kwin.at[last], load_sem.at[1]),
        pltpu.make_async_copy(v_hbm, vwin.at[last], load_sem.at[2]),
        pltpu.make_async_copy(e_hbm, entries, load_sem.at[3]),
    ]
    for load in loads:
        load.start()
    pl.semaphore_wait(barrier, len(peers))

    halos = []
    for reach in (1, 2):
        place = pl.ds((REACH - reach) * rows, rows)
        for which, (source, window) in enumerate(((k_hbm, kwin), (v_hbm, vwin))):
            halos.append(
                pltpu.make_async_remote_copy(
                    src_ref=source,
                    dst_ref=window.at[place],
                    send_sem=halo_send.at[reach - 1, which],
                    recv_sem=halo_recv.at[reach - 1, which],
                    device_id=ctx_at(reach),
                    device_id_type=MESH,
                )
            )

    def place_of(piece):
        group, block, first, heads = piece
        return pl.ds(block * BLOCK, BLOCK), pl.ds((group * SHARE + first) * SIZE, heads * SIZE)

    def grad_copy(index):
        part, lanes = place_of(PIECES[index])
        return pltpu.make_async_remote_copy(
            src_ref=g_hbm.at[part, lanes],
            dst_ref=gbuf.at[part, lanes],
            send_sem=grad_send.at[index],
            recv_sem=grad_recv.at[index],
            device_id=pipe_at(-1),
            device_id_type=MESH,
        )

    def msg_copy(group, block, reach):
        return pltpu.make_async_remote_copy(
            src_ref=msg.at[group, block],
            dst_ref=arrived.at[reach - 1, group, block],
            send_sem=msg_send.at[reach - 1, group, block],
            recv_sem=msg_recv.at[reach - 1, group, block],
            device_id=ctx_at(-reach),
            device_id_type=MESH,
        )

    note_copies = [
        pltpu.make_async_remote_copy(
            src_ref=note,
            dst_ref=notes.at[reach - 1],
            send_sem=note_send.at[reach - 1],
            recv_sem=note_recv.at[reach - 1],
            device_id=ctx_at(-reach),
            device_id_type=MESH,
        )
        for reach in (1, 2)
    ]

    grads = [grad_copy(index) for index in range(len(PIECES))]
    grads[0].start()
    for halo in halos:
        halo.start()
    for grad in grads[1:]:
        grad.start()
    for load in loads:
        load.wait()
    for halo in halos:
        halo.wait_recv()

    def slot_of(block, shape):
        entry = jnp.full(shape, entries[block, 1], jnp.int32)
        return jnp.where(entry >= 0, entry - (rank - REACH) * BLOCKS, -1)

    for block in range(BLOCKS):
        note[block] = slot_of(block, (8, SIZE))
    for copy in note_copies:
        copy.start()

    for block in range(BLOCKS):
        wide = slot_of(block, (BLOCK, narrow))
        for window, parents in ((kwin, kpar), (vwin, vpar)):
            total = jnp.zeros((BLOCK, narrow), jnp.float32)
            for slot in range(block, REACH * BLOCKS + block):
                held = window[pl.ds(slot * BLOCK, BLOCK), :].astype(jnp.float32)
                total = jnp.where(wide == slot, held, total)
            parents[block] = total.astype(jnp.bfloat16)

    def chosen(window, parents, group, block):
        lanes = pl.ds(pl.multiple_of(group * SIZE, SIZE), SIZE)
        mine = window[pl.ds(REACH * rows + block * BLOCK, BLOCK), lanes]
        return jnp.concatenate([mine, parents[block, :, lanes]], axis=0)

    slots = [slot_of(block, (BLOCK, SIZE)) for block in range(BLOCKS)]
    width = SHARE * BLOCK
    key_row = lax.broadcasted_iota(jnp.int32, (BLOCK, width), 0)
    query_row = lax.rem(lax.broadcasted_iota(jnp.int32, (BLOCK, width), 1), BLOCK)

    def forward(group, carry):
        for block in range(BLOCKS):
            scores = nt(chosen(kwin, kpar, group, block), stacked(qbuf, block, group))
            mine = jnp.where(key_row <= query_row, scores[:BLOCK], NEG)
            parent = jnp.where(slot_of(block, (BLOCK, width)) >= 0, scores[BLOCK:], NEG)
            top = jnp.maximum(
                jnp.max(mine, axis=0, keepdims=True), jnp.max(parent, axis=0, keepdims=True)
            )
            mine = jnp.exp((mine - top) * scale)
            parent = jnp.exp((parent - top) * scale)
            total = jnp.sum(mine, axis=0, keepdims=True) + jnp.sum(parent, axis=0, keepdims=True)
            inverse = 1.0 / total
            prob[group, block, :BLOCK] = mine * inverse
            prob[group, block, BLOCK:] = parent * inverse
        return carry

    lax.fori_loop(0, GROUPS, forward, 0)

    def backward(piece):
        group, block, first, heads = piece
        soft = prob[group, block, :, pl.ds(first * BLOCK, heads * BLOCK)]
        dprob = nt(chosen(vwin, vpar, group, block), stacked(gbuf, block, group, first, heads))
        dot = jnp.sum(soft * dprob, axis=0, keepdims=True)
        dscore = (soft * (dprob - dot)).astype(jnp.bfloat16)
        queries = stacked(qbuf, block, group, first, heads)
        return dscore, jnp.dot(dscore, queries, preferred_element_type=jnp.float32) * scale

    def query_part(piece, dscore):
        group, block, first, heads = piece
        dquery = (tn(dscore, chosen(kwin, kpar, group, block)) * scale).astype(jnp.bfloat16)
        for h in range(heads):
            dq_ref[pl.ds(block * BLOCK, BLOCK), pl.ds((group * SHARE + first + h) * SIZE, SIZE)] = (
                dquery[h * BLOCK : (h + 1) * BLOCK]
            )

    def close(group):
        parts = [own[group, :BLOCK], own[group, BLOCK:]]
        for reach in range(1, REACH + 1):
            for sent in range(BLOCKS):
                msg_copy(group, sent, reach).wait_recv()
                slot = jnp.broadcast_to(notes[reach - 1, sent, :1], (BLOCK, SIZE))
                part = arrived[reach - 1, group, sent].astype(jnp.float32)
                for mine in range(BLOCKS):
                    hit = slot == (REACH - reach) * BLOCKS + mine
                    parts[mine] = parts[mine] + jnp.where(hit, part, 0.0)
        for mine in range(BLOCKS):
            dk_ref[pl.ds(mine * BLOCK, BLOCK), pl.ds(group * SIZE, SIZE)] = parts[mine].astype(
                jnp.bfloat16
            )

    totals = {}
    for index, piece in enumerate(PIECES):
        group, block = piece[:2]
        grads[index].wait_recv()
        dscore, dkey = backward(piece)
        totals[block] = totals[block] + dkey if piece[2] else dkey
        if piece[2] + piece[3] == SHARE:
            parent = totals[block][BLOCK:]
            msg[group, block] = parent.astype(jnp.bfloat16)
            for reach in (2, 1):
                msg_copy(group, block, reach).start()
            own[group, pl.ds(block * BLOCK, BLOCK)] = totals[block][:BLOCK]
            if block:
                near = jnp.where(slots[block] == REACH * BLOCKS, parent, 0.0)
                own[group, :BLOCK] = own[group, :BLOCK] + near
        query_part(piece, dscore)
        if index + 2 == len(PIECES):
            for copy in note_copies:
                copy.wait_recv()
            for earlier in range(GROUPS - 1):
                close(earlier)

    for halo in halos:
        halo.wait_send()
    for copy in note_copies:
        copy.wait_send()
    for grad in grads:
        grad.wait_send()
    for group in range(GROUPS - 1):
        for sent in range(BLOCKS):
            for reach in (1, 2):
                msg_copy(group, sent, reach).wait_send()
    close(GROUPS - 1)
    for sent in range(BLOCKS):
        for reach in (1, 2):
            msg_copy(GROUPS - 1, sent, reach).wait_send()


def finish(dq_in, dk_in, dq_out, dk_out, sem):
    rows = dq_in.shape[0] // CUTS
    copies = [pltpu.make_async_copy(dk_in, dk_out, sem.at[CUTS])]
    for cut in range(CUTS):
        part = pl.ds(cut * rows, rows)
        copies.append(pltpu.make_async_copy(dq_in.at[part], dq_out.at[part], sem.at[cut]))
    for copy in copies:
        copy.start()
    for copy in copies:
        copy.wait()


def solution(mesh):
    pipes, ranks = mesh.shape["pipe"], mesh.shape["ctx"]

    def per_device(query, key, value, grad, key_blocks):
        rows = query.shape[1]
        wide, narrow = query.shape[2], key.shape[2]
        anywhere = pl.BlockSpec(memory_space=pl.ANY)
        dma = pltpu.SemaphoreType.DMA
        dq, dk = pl.pallas_call(
            functools.partial(kernel, pipes, ranks),
            out_shape=(
                jax.ShapeDtypeStruct((rows, wide), jnp.bfloat16),
                jax.ShapeDtypeStruct((rows, narrow), jnp.bfloat16),
            ),
            in_specs=[pl.BlockSpec(memory_space=pltpu.HBM)] * 5,
            out_specs=(pl.BlockSpec(memory_space=pltpu.VMEM),) * 2,
            scratch_shapes=[
                pltpu.SMEM((BLOCKS, 2), jnp.int32),
                pltpu.VMEM((rows, wide), jnp.bfloat16),
                pltpu.VMEM((rows, wide), jnp.bfloat16),
                pltpu.VMEM(((REACH + 1) * rows, narrow), jnp.bfloat16),
                pltpu.VMEM(((REACH + 1) * rows, narrow), jnp.bfloat16),
                pltpu.VMEM((BLOCKS, BLOCK, narrow), jnp.bfloat16),
                pltpu.VMEM((BLOCKS, BLOCK, narrow), jnp.bfloat16),
                pltpu.VMEM((GROUPS, BLOCKS, 2 * BLOCK, SHARE * BLOCK), jnp.float32),
                pltpu.VMEM((GROUPS, rows, SIZE), jnp.float32),
                pltpu.VMEM((GROUPS, BLOCKS, BLOCK, SIZE), jnp.bfloat16),
                pltpu.VMEM((REACH, GROUPS, BLOCKS, BLOCK, SIZE), jnp.bfloat16),
                pltpu.VMEM((BLOCKS, 8, SIZE), jnp.int32),
                pltpu.VMEM((REACH, BLOCKS, 8, SIZE), jnp.int32),
                dma((4,)),
                dma((REACH, 2)),
                dma((REACH, 2)),
                dma((len(PIECES),)),
                dma((len(PIECES),)),
                dma((REACH, GROUPS, BLOCKS)),
                dma((REACH, GROUPS, BLOCKS)),
                dma((REACH,)),
                dma((REACH,)),
            ],
            compiler_params=pltpu.CompilerParams(
                collective_id=0, has_side_effects=True, vmem_limit_bytes=32 * 1024 * 1024
            ),
            cost_estimate=pl.CostEstimate(
                flops=700_000_000, bytes_accessed=4_000_000, transcendentals=600_000
            ),
        )(*[pltpu.with_memory_space_constraint(x[0], pltpu.HBM) for x in (key_blocks, query, key, value, grad)])
        dq, dk = pl.pallas_call(
            finish,
            out_shape=(
                jax.ShapeDtypeStruct((rows, wide), jnp.bfloat16),
                jax.ShapeDtypeStruct((rows, narrow), jnp.bfloat16),
            ),
            in_specs=[anywhere] * 2,
            out_specs=[pl.BlockSpec(memory_space=pltpu.HBM)] * 2,
            scratch_shapes=[dma((CUTS + 1,))],
            compiler_params=pltpu.CompilerParams(vmem_limit_bytes=4 * 1024 * 1024),
        )(*[pltpu.with_memory_space_constraint(x, pltpu.VMEM) for x in (dq, dk)])
        return dq[None], dk[None]

    spec = P("pipe", "ctx", None)
    return jax.shard_map(
        per_device, mesh=mesh, in_specs=(spec,) * 5, out_specs=(spec, spec), check_vma=False
    )
```
